32 devices in a mesh: rep: 2 (over core), dom: 16 (over z, y, x).
Axes of the slice: x: 2, y: 2, z: 4, core: 2. Of those that a mesh axis runs over, the one named last changes fastest.
Arguments:
- features: bfloat16 [2048, 512], P('dom'), may hold values from -6 to 6
- tiles: bfloat16 [2048, 128, 128], P(('rep', 'dom')), may hold values from -0.359375 to 0.359375
- tile_dest: int32 [2048, 1], P(('rep', 'dom')), may hold values from 0 to 15; in each aligned block of 64 rows (0 to 63, 64 to 127, ...) at most 8 rows name the same one
- tile_count: int32 [2048], P(('rep', 'dom')), may hold values from 16 to 128
- weight: bfloat16 [512, 512], replicated, may hold values from -0.25 to 0.25
- bias: float32 [512], replicated, may hold values from -3 to 3
- cotangent: bfloat16 [2048, 512], P('dom'), may hold values from -6 to 6
Outputs:
- activated: bfloat16 [2048, 512], P('dom', 'rep')
- weight_grad: float32 [512, 512], P(None, 'rep')
- feature_grad: bfloat16 [2048, 512], P('dom', 'rep')
The draws below stay inside these ranges and needn't reach their ends.
Inputs may be any that keep to these rules, and one draw needn't show every extreme that they name: `tile_dest`: among the tiles of one device no block is named more than 8 times, and some block is named exactly 8 times.
All inputs are finite; a program needn't handle non-finite values.
Results may differ from the reference program's by a relative error of at most 0.02.
Values may be sent and summed in bfloat16 or wider, within the bound.
No kernel may reach another device: no remote copies, remote signals or barrier semaphores. Data moves between devices by JAX's collectives and lax.ppermute only.
A program may use at most 128 MiB of HBM per device.

```python
import math
import jax
import jax.numpy as jnp
import numpy as np
from jax import lax

F = 512
BLK = 128
TILES_DEV = 64
CAP = 8
NODES = 2048
TILES = 2048
N_DOM = 16


def with_ends(drawn, rng, least, high):
    spot = [jax.random.randint(jax.random.fold_in(rng, axis), (), 0, length) for axis, length in enumerate(drawn.shape)]
    main_axis = drawn.shape.index(max(drawn.shape))
    next_to = spot[:main_axis] + [(spot[main_axis] + 1) % drawn.shape[main_axis]] + spot[main_axis + 1:]
    return drawn.at[tuple(spot)].set(least).at[tuple(next_to)].set(high)


def shard_levels(own_key, shape, pieces, low, top_value):
    def one(position, shards_of):
        steps = jax.random.uniform(jax.random.fold_in(jax.random.fold_in(own_key, 6), position), (shards_of,), jnp.float32, low / len(pieces), top_value / len(pieces))
        return jnp.repeat(jnp.exp(steps), shape[position] // shards_of).reshape((-1,) + (1,) * (len(shape) - position - 1))

    loudness = one(*pieces[0])
    for cut in pieces[1:]:
        loudness = loudness * one(*cut)
    return loudness


def deal_out(stream_key, own, number, rows, number_of, top, bound, lean):
    ranking = jax.random.permutation(stream_key, number_of)
    packed, usual = load_shares(number_of, rows * top, bound, lean, True), load_shares(number_of, rows * top, bound, lean, False)
    places = jnp.arange(number_of)

    def named(lengths, rotation):
        used = int((lengths > 0).sum())
        fixed = max(1, used // 4)
        moved = fixed + (places - fixed + rotation * (used - fixed)) % max(1, number_of - fixed)
        return jnp.zeros((number_of,), jnp.int32).at[ranking[jnp.where(places < fixed, places, moved)]].set(jnp.asarray(lengths, jnp.int32))

    lengths = jnp.where(number % 4 == 0, named(packed, number // 4), named(usual, number - number // 4 - 1))
    mixed = jax.random.permutation(jax.random.fold_in(own, 3), number_of)
    giver, receiver = mixed[0:number_of // 2 * 2:2], mixed[1:number_of // 2 * 2:2]
    slack = jnp.minimum(lengths[giver] - 1, bound - lengths[receiver]) // 2
    slack = jnp.where((giver == ranking[0]) | (receiver == ranking[0]) | (lengths[receiver] == 0), 0, jnp.maximum(slack, 0))
    moved = jax.random.randint(jax.random.fold_in(own, 4), (number_of // 2,), 0, 1 << 20) % (slack + 1)
    lengths = lengths.at[giver].add(-moved).at[receiver].add(moved)
    items = jnp.searchsorted(jnp.cumsum(lengths), jnp.arange(rows * top), side="right").astype(jnp.int32)
    grid = items.reshape(top, rows).T
    grid = grid[jax.random.permutation(jax.random.fold_in(own, 1), rows)]
    rotation = jax.random.randint(jax.random.fold_in(own, 2), (rows, 1), 0, top)
    return jnp.take_along_axis(grid, (jnp.arange(top)[None, :] + rotation) % top, axis=1)


def load_shares(number_of, total, limit, slope, full):
    portions = [(1 << 20) // math.isqrt(rank ** slope) + 1 for rank in range(1, number_of + 1)]
    largest = limit if full else min(limit, max(-(-total // number_of), total * portions[0] // sum(portions)))
    least = 1 if total - largest >= number_of - 1 else 0
    given, surplus = [largest] + [least] * (number_of - 1), total - largest - least * (number_of - 1)
    while surplus > 0:
        candidates = [i for i in range(1, number_of) if given[i] < largest] or [i for i in range(1, number_of) if given[i] < limit]
        pool, remaining = sum([portions[i] for i in candidates]), surplus
        for i in candidates:
            more = min(limit - given[i], max(1, remaining * portions[i] // pool), surplus)
            given[i] = given[i] + more
            surplus = surplus - more
    return np.array(given)


def gaussian(stream_key, shape, deviation, most, cuts=(), held_as=jnp.bfloat16):
    drawn = jax.random.normal(stream_key, shape, jnp.float32) * deviation
    if len(cuts) > 0:
        drawn = shard_levels(stream_key, shape, cuts, -0.22, 0.18) * drawn
    return jnp.clip(drawn, min=-most, max=most).astype(held_as)


def setup_inputs(seed: int = 0) -> dict:
    key_list = jax.random.split(jax.random.key(seed), 8)
    features = gaussian(key_list[0], (NODES, F), 1.0, 6.0, ((0, 16),))
    tiles = gaussian(key_list[1], (TILES, BLK, BLK), 0.06, 0.359375, ((0, 32),))
    tile_dest_keys = jax.random.split(jax.random.fold_in(key_list[2], 1), TILES // TILES_DEV)
    tile_dest_turns = jax.random.permutation(jax.random.fold_in(key_list[2], 3), TILES // TILES_DEV)
    tile_dest = jax.vmap(lambda own, number: deal_out(jax.random.fold_in(key_list[2], 2), own, number, TILES_DEV, N_DOM, 1, CAP, 1))(tile_dest_keys, tile_dest_turns).reshape((TILES, 1))
    tile_count = with_ends(jax.random.randint(key_list[3], (TILES,), 16, 129), jax.random.fold_in(key_list[3], 1), 16, 128).astype(jnp.int32)
    weight = gaussian(key_list[4], (F, F), F ** -0.5, 0.25)
    bias = gaussian(key_list[5], (F,), 0.5, 3.0, (), jnp.float32)
    cotangent = gaussian(key_list[6], (NODES, F), 1.0, 6.0, ((0, 16),))
    return {"features": features, "tiles": tiles, "tile_dest": tile_dest, "tile_count": tile_count, "weight": weight, "bias": bias, "cotangent": cotangent}


def reference(features, tiles, tile_dest, tile_count, weight, bias, cotangent):
    shards = 2 * N_DOM
    blocks = features.reshape(N_DOM, BLK, F).astype(jnp.float32)
    tile_sets = tiles.reshape(shards, TILES_DEV, BLK, BLK)
    dest_sets = tile_dest.reshape(shards, TILES_DEV).astype(jnp.int32)
    scale_sets = lax.rsqrt(tile_count.astype(jnp.float32)).reshape(shards, TILES_DEV)
    source_ids = (jnp.arange(shards, dtype=jnp.int32) % N_DOM).astype(jnp.int32)

    def forward_step(total, item):
        tile_set, dest_set, scale_set, source = item
        panel = blocks[source]
        terms = jnp.einsum('tij,jf->tif', tile_set.astype(jnp.float32), panel) * scale_set[:, None, None]
        rounded = lax.optimization_barrier(terms.astype(jnp.bfloat16))
        return (total.at[dest_set].add(rounded.astype(jnp.float32)), None)
    start = jnp.zeros((N_DOM, BLK, F), jnp.float32)
    summed, _ = lax.scan(forward_step, start, (tile_sets, dest_sets, scale_sets, source_ids))
    aggregated = summed.reshape(NODES, F).astype(jnp.bfloat16)
    pre = jnp.dot(aggregated, weight, preferred_element_type=jnp.float32) + bias
    sig = jax.nn.sigmoid(pre)
    activated = (pre * sig).astype(jnp.bfloat16)
    pre_grad = (cotangent.astype(jnp.float32) * sig * (1.0 + pre * (1.0 - sig))).astype(jnp.bfloat16)
    weight_grad = jnp.dot(aggregated.T, pre_grad, preferred_element_type=jnp.float32) / jnp.sqrt(jnp.float32(NODES))
    row_grad = jnp.dot(pre_grad, weight.T, preferred_element_type=jnp.float32).astype(jnp.bfloat16)
    grad_blocks = row_grad.reshape(N_DOM, BLK, F).astype(jnp.float32)

    def backward_step(total, item):
        tile_set, dest_set, scale_set, source = item
        picked = grad_blocks[dest_set]
        terms = jnp.einsum('tij,tif->tjf', tile_set.astype(jnp.float32), picked) * scale_set[:, None, None]
        return (total.at[source].add(lax.optimization_barrier(jnp.sum(terms, axis=0))), None)
    back, _ = lax.scan(backward_step, jnp.zeros((N_DOM, BLK, F), jnp.float32), (tile_sets, dest_sets, scale_sets, source_ids))
    feature_grad = back.reshape(NODES, F).astype(jnp.bfloat16)
    return (activated, weight_grad, feature_grad)
```

```python
import functools
import math

import jax
import jax.numpy as jnp
from jax import lax
from jax.experimental import pallas as pl
from jax.experimental.pallas import tpu as pltpu
from jax.sharding import PartitionSpec as P

F32, BF16 = jnp.float32, jnp.bfloat16
VMEM_LIMIT = 48 * 1024 * 1024


def place(group):
    dom = lax.axis_index("dom")
    return lax.axis_index("rep"), lax.div(dom, group), lax.rem(dom, group)


def rows(start, size):
    return pl.ds(pl.multiple_of(start * size, size), size)


def call(kernel, outs, scratch=(), smem=0, args=()):
    spec = pl.BlockSpec(memory_space=pltpu.VMEM)
    return pl.pallas_call(
        kernel,
        out_shape=[jax.ShapeDtypeStruct(shape, dtype) for shape, dtype in outs],
        in_specs=[pl.BlockSpec(memory_space=pltpu.SMEM)] * smem + [spec] * (len(args) - smem),
        out_specs=[spec] * len(outs),
        scratch_shapes=list(scratch),
        compiler_params=pltpu.CompilerParams(vmem_limit_bytes=VMEM_LIMIT),
    )(*args)


def combine_kernel(per_step, dest_ref, count_ref, tiles_ref, own_ref, send_ref, total):
    step = pl.program_id(0)
    half = total.shape[1] // 2

    @pl.when(step == 0)
    def _():
        total[...] = jnp.zeros_like(total)

    def add(i, carry):
        t = step * per_step + i
        count = jnp.full((1, total.shape[2]), count_ref[t], jnp.int32)
        scale = lax.rsqrt(count.astype(F32))
        d = dest_ref[t]
        total[d] = total[d] + tiles_ref[i].astype(F32) * scale
        return carry

    lax.fori_loop(0, per_step, add, 0, unroll=2)

    @pl.when(step == pl.num_programs(0) - 1)
    def _():
        rep = lax.axis_index("rep")
        own_ref[...] = total[:, rows(rep, half), :].astype(BF16)
        send_ref[...] = total[:, rows(1 - rep, half), :].astype(BF16)


def combine(dest, count, tiles, domains):
    number, block, _ = tiles.shape
    per_step = number // 4
    half = (domains, block // 2, block)
    whole = lambda i: (0, 0, 0)
    return pl.pallas_call(
        functools.partial(combine_kernel, per_step),
        grid=(number // per_step,),
        out_shape=[jax.ShapeDtypeStruct(half, BF16)] * 2,
        in_specs=[
            pl.BlockSpec(memory_space=pltpu.SMEM),
            pl.BlockSpec(memory_space=pltpu.SMEM),
            pl.BlockSpec((per_step, block, block), lambda i: (i, 0, 0)),
        ],
        out_specs=[pl.BlockSpec(half, whole)] * 2,
        scratch_shapes=[pltpu.VMEM((domains, block, block), F32)],
        compiler_params=pltpu.CompilerParams(vmem_limit_bytes=VMEM_LIMIT),
    )(dest, count, tiles)


def split_kernel(group, own_ref, got_ref, features_ref, *outs):
    rep, _, q = place(group)
    outer = own_ref.shape[0] // group
    for s in range(group):
        for z in range(outer):
            b = z * group + lax.bitwise_xor(q, s)
            outs[s][z] = (own_ref[b].astype(F32) + got_ref[b].astype(F32)).astype(BF16)
    width = features_ref.shape[1] // 2
    outs[group][...] = features_ref[:, rows(rep, width)]


def forward_kernel(group, *refs):
    own, got = refs[:group], refs[group : 2 * group]
    features = refs[2 * group : 3 * group]
    adjacency = refs[3 * group]
    outs = refs[3 * group + 1 :]
    rep, z, _ = place(group)
    outer, half, block = own[0].shape
    for t in range(outer):
        far = lax.bitwise_xor(z, t)
        for s in range(group):
            columns = slice(s * block, (s + 1) * block)
            adjacency[t, rows(rep, half), columns] = own[s][far]
            adjacency[t, rows(1 - rep, half), columns] = got[s][far]
    panel = jnp.concatenate([f[...] for f in features], axis=0)
    for t in range(outer):
        part = jnp.dot(adjacency[t], panel, preferred_element_type=F32)
        outs[t][...] = part.astype(outs[t].dtype)


def sum_kernel(scale, *refs):
    out = refs[-1]
    total = refs[0][...].astype(F32)
    for ref in refs[1:-1]:
        total = total + ref[...].astype(F32)
    out[...] = (total * scale if scale is not None else total).astype(out.dtype)


def dense_kernel(group, own_ref, got_ref, weight_ref, bias_ref, cotangent_ref, *refs):
    active_ref, row_grad_ref = refs[:2]
    outs = refs[2 : 2 + group]
    agg, pre_ref, grad, parts = refs[2 + group :]
    rep, _, q = place(group)
    width = own_ref.shape[1]
    agg[:, rows(rep, width)] = own_ref[...]
    agg[:, rows(1 - rep, width)] = got_ref[...]
    pre = jnp.dot(agg[...], weight_ref[...], preferred_element_type=F32) + bias_ref[...]
    sig = jax.nn.sigmoid(pre)
    pre_ref[...] = pre * sig
    active_ref[...] = pre_ref[:, rows(rep, width)].astype(BF16)
    slope = cotangent_ref[...].astype(F32) * sig * (1.0 + pre * (1.0 - sig))
    grad[...] = slope.astype(BF16)
    row_grad = lax.dot_general(
        grad[...], weight_ref[rows(rep, width), :], (((1,), (1,)), ((), ())), preferred_element_type=F32
    )
    row_grad_ref[...] = row_grad.astype(BF16)
    parts[...] = lax.dot_general(
        agg[...], grad[:, rows(rep, width)], (((0,), (0,)), ((), ())), preferred_element_type=F32
    )
    size = parts.shape[0] // group
    for s in range(group):
        outs[s][...] = parts[rows(lax.bitwise_xor(q, s), size), :].astype(outs[s].dtype)


def backward_kernel(group, adjacency, *refs):
    outer, block, _ = adjacency.shape
    grads, outs = refs[:outer], refs[outer:]
    for s in range(group):
        columns = slice(s * block, (s + 1) * block)
        total = jnp.zeros(outs[s].shape, F32)
        for t in range(outer):
            total = total + lax.dot_general(
                adjacency[t, :, columns], grads[t][...], (((0,), (0,)), ((), ())), preferred_element_type=F32
            )
        outs[s][...] = total.astype(outs[s].dtype)


def assemble_kernel(group, *refs):
    out = refs[-1]
    _, _, q = place(group)
    size = refs[0].shape[0]
    for s in range(group):
        out[rows(lax.bitwise_xor(q, s), size), :] = refs[s][...].astype(F32)


def per_device(features, tiles, tile_dest, tile_count, weight, bias, cotangent):
    domains = lax.axis_size("dom")
    group = 4
    outer = domains // group
    block, width = features.shape
    half = width // 2
    nodes = domains * block

    def rep_swap(x):
        return lax.ppermute(x, "rep", [(0, 1), (1, 0)])

    def inner_swap(x, s):
        return lax.ppermute(x, "dom", [(i, i ^ s) for i in range(domains)])

    def outer_swap(x, t):
        return lax.ppermute(x, "dom", [(i, i ^ (t * group)) for i in range(domains)])

    own, send = combine(tile_dest[:, 0], tile_count, tiles, domains)
    got = rep_swap(send)
    *cut, panel = call(
        functools.partial(split_kernel, group),
        [((outer, block // 2, block), BF16)] * group + [((block, half), BF16)],
        args=(own, got, features),
    )
    mine = [cut[0]] + [inner_swap(cut[s], s) for s in range(1, group)]
    panels = [panel] + [inner_swap(panel, s) for s in range(1, group)]
    others = [rep_swap(x) for x in mine]
    adjacency, *parts = call(
        functools.partial(forward_kernel, group),
        [((outer, block, group * block), BF16), ((block, half), F32)] + [((block, half), BF16)] * (outer - 1),
        args=(*mine, *others, *panels),
    )
    parts = [parts[0]] + [outer_swap(parts[t], t) for t in range(1, outer)]
    (agg,) = call(functools.partial(sum_kernel, None), [((block, half), BF16)], args=parts)
    activated, row_grad, *pieces = call(
        functools.partial(dense_kernel, group),
        [((block, half), BF16), ((block, half), BF16), ((width // group, half), F32)]
        + [((width // group, half), BF16)] * (group - 1),
        scratch=(
            pltpu.VMEM((block, width), BF16),
            pltpu.VMEM((block, width), F32),
            pltpu.VMEM((block, width), BF16),
            pltpu.VMEM((width, half), F32),
        ),
        args=(agg, rep_swap(agg), weight, bias.reshape(1, width), cotangent),
    )
    grads = [row_grad] + [outer_swap(row_grad, t) for t in range(1, outer)]
    pieces = [pieces[0]] + [inner_swap(pieces[s], s) for s in range(1, group)]
    back = call(
        functools.partial(backward_kernel, group),
        [((block, half), F32)] + [((block, half), BF16)] * (group - 1),
        args=(adjacency, *grads),
    )
    back = [back[0]] + [inner_swap(back[s], s) for s in range(1, group)]
    (piece,) = call(functools.partial(sum_kernel, None), [((width // group, half), BF16)], args=pieces)
    pieces = [piece] + [outer_swap(piece, t) for t in range(1, outer)]
    (piece,) = call(
        functools.partial(sum_kernel, 1.0 / math.sqrt(nodes)), [((width // group, half), BF16)], args=pieces
    )
    pieces = [piece] + [inner_swap(piece, s) for s in range(1, group)]
    (weight_grad,) = call(functools.partial(assemble_kernel, group), [((width, half), F32)], args=pieces)
    (feature_grad,) = call(functools.partial(sum_kernel, None), [((block, half), BF16)], args=back)
    return (activated, weight_grad, feature_grad)


def solution(mesh):
    in_specs = (
        P("dom", None),
        P(("rep", "dom"), None, None),
        P(("rep", "dom"), None),
        P(("rep", "dom")),
        P(),
        P(),
        P("dom", None),
    )
    out_specs = (P("dom", "rep"), P(None, "rep"), P("dom", "rep"))
    return jax.shard_map(
        per_device, mesh=mesh, in_specs=in_specs, out_specs=out_specs, check_vma=False
    )
```

```python
import functools
import math

import jax
import jax.numpy as jnp
from jax import lax
from jax.experimental import pallas as pl
from jax.experimental.pallas import tpu as pltpu
from jax.sharding import PartitionSpec as P

F32, BF16 = jnp.float32, jnp.bfloat16
VMEM_LIMIT = 48 * 1024 * 1024
SHORT = pl.CostEstimate(flops=1024, bytes_accessed=1024, transcendentals=0)
CHUNKS = 4


def place(group):
    dom = lax.axis_index("dom")
    return lax.axis_index("rep"), lax.div(dom, group), lax.rem(dom, group)


def rows(start, size):
    return pl.ds(pl.multiple_of(start * size, size), size)


def call(kernel, outs, scratch=(), smem=0, args=()):
    spec = pl.BlockSpec(memory_space=pltpu.VMEM)
    return pl.pallas_call(
        kernel,
        out_shape=[jax.ShapeDtypeStruct(shape, dtype) for shape, dtype in outs],
        in_specs=[pl.BlockSpec(memory_space=pltpu.SMEM)] * smem + [spec] * (len(args) - smem),
        out_specs=[spec] * len(outs),
        scratch_shapes=list(scratch),
        compiler_params=pltpu.CompilerParams(vmem_limit_bytes=VMEM_LIMIT),
        cost_estimate=SHORT,
    )(*args)


def combine_kernel(dest_hbm, count_hbm, tiles_hbm, own_ref, send_ref, total, tiles, dest, count, sems):
    half = total.shape[1] // 2
    size = tiles.shape[0] // CHUNKS
    copies = [
        pltpu.make_async_copy(dest_hbm, dest, sems.at[CHUNKS]),
        pltpu.make_async_copy(count_hbm, count, sems.at[CHUNKS + 1]),
    ]
    for c in range(CHUNKS):
        part = pl.ds(c * size, size)
        copies.append(pltpu.make_async_copy(tiles_hbm.at[part], tiles.at[part], sems.at[c]))
    for copy in copies:
        copy.start()
    total[...] = jnp.zeros_like(total)
    copies[0].wait()
    copies[1].wait()

    def add(t, carry):
        scale = lax.rsqrt(jnp.full((1, total.shape[2]), count[t], jnp.int32).astype(F32))
        d = dest[t]
        total[d] = total[d] + tiles[t].astype(F32) * scale
        return carry

    for c in range(CHUNKS):
        copies[2 + c].wait()
        lax.fori_loop(c * size, (c + 1) * size, add, 0, unroll=2)
    rep = lax.axis_index("rep")
    own_ref[...] = total[:, rows(rep, half), :].astype(BF16)
    send_ref[...] = total[:, rows(1 - rep, half), :].astype(BF16)


def combine(dest, count, tiles, domains):
    number, block, _ = tiles.shape
    half = (domains, block // 2, block)
    return pl.pallas_call(
        combine_kernel,
        out_shape=[jax.ShapeDtypeStruct(half, BF16)] * 2,
        in_specs=[pl.BlockSpec(memory_space=pltpu.HBM)] * 3,
        out_specs=[pl.BlockSpec(memory_space=pltpu.VMEM)] * 2,
        scratch_shapes=[
            pltpu.VMEM((domains, block, block), F32),
            pltpu.VMEM(tiles.shape, BF16),
            pltpu.SMEM((number,), jnp.int32),
            pltpu.SMEM((number,), jnp.int32),
            pltpu.SemaphoreType.DMA((CHUNKS + 2,)),
        ],
        compiler_params=pltpu.CompilerParams(vmem_limit_bytes=VMEM_LIMIT),
        cost_estimate=SHORT,
    )(*[pltpu.with_memory_space_constraint(x, pltpu.HBM) for x in (dest, count, tiles)])


def split_kernel(group, near, own_ref, got_ref, features_ref, *outs):
    rep, _, q = place(group)
    outer = own_ref.shape[0] // group
    _, half, block = own_ref.shape
    for i, s in enumerate(near):
        for z in range(outer):
            b = z * group + lax.bitwise_xor(q, s)
            outs[i][z * half : (z + 1) * half] = (own_ref[b].astype(F32) + got_ref[b].astype(F32)).astype(BF16)
    parts = features_ref.shape[1] // 2 // block
    for i in range(parts):
        piece = features_ref[:, rows(rep * parts + i, block)]
        at = outer * half + i * block
        for s in range(1, group):
            outs[s][at : at + block] = piece


def forward_kernel(group, outer, near, far, *refs):
    own = [refs[near.index(s)] for s in range(group)]
    got = [refs[group + near.index(s)] for s in range(group)]
    features_ref, adjacency = refs[2 * group : 2 * group + 2]
    outs, panel = refs[2 * group + 2 : -1], refs[-1]
    rep, z, _ = place(group)
    block, width = features_ref.shape
    half, side = block // 2, width // 2
    for t in range(outer):
        at = pl.ds(pl.multiple_of(lax.bitwise_xor(z, t) * half, half), half)
        for s in range(group):
            columns = slice(s * block, (s + 1) * block)
            adjacency[t, rows(rep, half), columns] = own[s][at, :]
            adjacency[t, rows(1 - rep, half), columns] = got[s][at, :]
    panel[:block, :] = features_ref[:, rows(rep, side)]
    for s in range(1, group):
        for i in range(side // block):
            start = outer * half + i * block
            panel[s * block : (s + 1) * block, i * block : (i + 1) * block] = own[s][start : start + block, :]
    for i, t in enumerate(far):
        part = jnp.dot(adjacency[t], panel[...], preferred_element_type=F32)
        outs[i][...] = part.astype(outs[i].dtype)


def sum_kernel(scale, *refs):
    out = refs[-1]
    total = refs[0][...].astype(F32)
    for ref in refs[1:-1]:
        total = total + ref[...].astype(F32)
    out[...] = (total * scale if scale is not None else total).astype(out.dtype)


def dense_kernel(group, near, own_ref, got_ref, weight_ref, bias_ref, cotangent_ref, *refs):
    active_ref, row_grad_ref = refs[:2]
    outs = refs[2 : 2 + group]
    agg, pre_ref, grad, parts = refs[2 + group :]
    rep, _, q = place(group)
    width = own_ref.shape[1]
    agg[:, rows(rep, width)] = own_ref[...]
    agg[:, rows(1 - rep, width)] = got_ref[...]
    pre = jnp.dot(agg[...], weight_ref[...], preferred_element_type=F32) + bias_ref[...]
    sig = jax.nn.sigmoid(pre)
    pre_ref[...] = pre * sig
    active_ref[...] = pre_ref[:, rows(rep, width)].astype(BF16)
    slope = cotangent_ref[...].astype(F32) * sig * (1.0 + pre * (1.0 - sig))
    grad[...] = slope.astype(BF16)
    row_grad = lax.dot_general(
        grad[...], weight_ref[rows(rep, width), :], (((1,), (1,)), ((), ())), preferred_element_type=F32
    )
    row_grad_ref[...] = row_grad.astype(BF16)
    parts[...] = lax.dot_general(
        agg[...], grad[:, rows(rep, width)], (((0,), (0,)), ((), ())), preferred_element_type=F32
    )
    size = parts.shape[0] // group
    for i, s in enumerate(near):
        outs[i][...] = parts[rows(lax.bitwise_xor(q, s), size), :].astype(outs[i].dtype)


def backward_kernel(group, near, far, adjacency, *refs):
    outer, block, _ = adjacency.shape
    grads, outs = refs[:outer], refs[outer:]
    for i, s in enumerate(near):
        columns = slice(s * block, (s + 1) * block)
        total = jnp.zeros(outs[i].shape, F32)
        for j, t in enumerate(far):
            total = total + lax.dot_general(
                adjacency[t, :, columns], grads[j][...], (((0,), (0,)), ((), ())), preferred_element_type=F32
            )
        outs[i][...] = total.astype(outs[i].dtype)


def assemble_kernel(near, *refs):
    out = refs[-1]
    _, _, q = place(len(near))
    size = refs[0].shape[0]
    for i, s in enumerate(near):
        out[rows(lax.bitwise_xor(q, s), size), :] = refs[i][...].astype(F32)


def per_device(features, tiles, tile_dest, tile_count, weight, bias, cotangent):
    domains = lax.axis_size("dom")
    group = 4
    outer = domains // group
    block, width = features.shape
    half = width // 2
    nodes = domains * block

    near = [0, group - 1, *range(1, group - 1)]
    far = [0, *range(outer // 2, outer), *range(1, outer // 2)]

    near_back, far_back = [0, *near[:0:-1]], [0, *far[:0:-1]]

    def rep_swap(x):
        return lax.ppermute(x, "rep", [(0, 1), (1, 0)])

    def inner_swap(x, s):
        return lax.ppermute(x, "dom", [(i, i ^ s) for i in range(domains)])

    def outer_swap(x, t):
        return lax.ppermute(x, "dom", [(i, i ^ (t * group)) for i in range(domains)])

    own, send = combine(tile_dest[:, 0], tile_count, tiles, domains)
    cut_rows = outer * block // 2
    cut = call(
        functools.partial(split_kernel, group, near),
        [((cut_rows, block), BF16)] + [((cut_rows + half, block), BF16)] * (group - 1),
        args=(own, rep_swap(send), features),
    )
    mine = [inner_swap(cut[i], s) if s else cut[i] for i, s in enumerate(near)]
    others = [rep_swap(x) for x in mine]
    adjacency, *parts = call(
        functools.partial(forward_kernel, group, outer, near, far),
        [((outer, block, group * block), BF16), ((block, half), F32)] + [((block, half), BF16)] * (outer - 1),
        scratch=(pltpu.VMEM((group * block, half), BF16),),
        args=(*mine, *others, features),
    )
    parts = [outer_swap(parts[i], t) if t else parts[i] for i, t in enumerate(far)]
    (agg,) = call(functools.partial(sum_kernel, None), [((block, half), BF16)], args=parts)
    activated, row_grad, *pieces = call(
        functools.partial(dense_kernel, group, near),
        [((block, half), BF16), ((block, half), BF16), ((width // group, half), F32)]
        + [((width // group, half), BF16)] * (group - 1),
        scratch=(
            pltpu.VMEM((block, width), BF16),
            pltpu.VMEM((block, width), F32),
            pltpu.VMEM((block, width), BF16),
            pltpu.VMEM((width, half), F32),
        ),
        args=(agg, rep_swap(agg), weight, bias.reshape(1, width), cotangent),
    )
    pieces = [inner_swap(pieces[i], s) if s else pieces[i] for i, s in enumerate(near)]
    (piece,) = call(functools.partial(sum_kernel, None), [((width // group, half), BF16)], args=pieces)
    grads = [outer_swap(row_grad, t) if t else row_grad for t in far_back]
    back = call(
        functools.partial(backward_kernel, group, near, far_back),
        [((block, half), F32)] + [((block, half), BF16)] * (group - 1),
        args=(adjacency, *grads),
    )
    back = [inner_swap(back[i], s) if s else back[i] for i, s in enumerate(near)]
    pieces = [outer_swap(piece, t) if t else piece for t in far_back]
    (piece,) = call(
        functools.partial(sum_kernel, 1.0 / math.sqrt(nodes)), [((width // group, half), BF16)], args=pieces
    )
    pieces = [inner_swap(piece, s) if s else piece for s in near_back]
    (weight_grad,) = call(functools.partial(assemble_kernel, near_back), [((width, half), F32)], args=pieces)
    (feature_grad,) = call(functools.partial(sum_kernel, None), [((block, half), BF16)], args=back)
    return (activated, weight_grad, feature_grad)


def solution(mesh):
    in_specs = (
        P("dom", None),
        P(("rep", "dom"), None, None),
        P(("rep", "dom"), None),
        P(("rep", "dom")),
        P(),
        P(),
        P("dom", None),
    )
    out_specs = (P("dom", "rep"), P(None, "rep"), P("dom", "rep"))
    return jax.shard_map(
        per_device, mesh=mesh, in_specs=in_specs, out_specs=out_specs, check_vma=False
    )
```

```python
import functools
import math

import jax
import jax.numpy as jnp
from jax import lax
from jax.experimental import pallas as pl
from jax.experimental.pallas import tpu as pltpu
from jax.sharding import PartitionSpec as P

F32, BF16 = jnp.float32, jnp.bfloat16
VMEM_LIMIT = 48 * 1024 * 1024
SHORT = pl.CostEstimate(flops=1024, bytes_accessed=1024, transcendentals=0)
CHUNKS = 4


def place(group):
    dom = lax.axis_index("dom")
    return lax.axis_index("rep"), lax.div(dom, group), lax.rem(dom, group)


def rows(start, size):
    return pl.ds(pl.multiple_of(start * size, size), size)


def call(kernel, outs, scratch=(), smem=0, args=()):
    spec = pl.BlockSpec(memory_space=pltpu.VMEM)
    return pl.pallas_call(
        kernel,
        out_shape=[jax.ShapeDtypeStruct(shape, dtype) for shape, dtype in outs],
        in_specs=[pl.BlockSpec(memory_space=pltpu.SMEM)] * smem + [spec] * (len(args) - smem),
        out_specs=[spec] * len(outs),
        scratch_shapes=list(scratch),
        compiler_params=pltpu.CompilerParams(vmem_limit_bytes=VMEM_LIMIT),
        cost_estimate=SHORT,
    )(*args)


def combine_kernel(mine, dest_hbm, count_hbm, tiles_hbm, out_ref, total, tiles, dest, count, sems):
    rep = lax.axis_index("rep")
    size = tiles.shape[0] // CHUNKS
    part = rows(rep if mine else 1 - rep, tiles.shape[1])
    copies = [
        pltpu.make_async_copy(dest_hbm, dest, sems.at[CHUNKS]),
        pltpu.make_async_copy(count_hbm, count, sems.at[CHUNKS + 1]),
    ]
    for c in range(CHUNKS):
        chunk = pl.ds(c * size, size)
        copies.append(pltpu.make_async_copy(tiles_hbm.at[chunk, part, :], tiles.at[chunk], sems.at[c]))
    for copy in copies:
        copy.start()
    total[...] = jnp.zeros_like(total)
    copies[0].wait()
    copies[1].wait()

    def add(t, carry):
        scale = lax.rsqrt(jnp.full((1, total.shape[2]), count[t], jnp.int32).astype(F32))
        d = dest[t]
        total[d] = total[d] + tiles[t].astype(F32) * scale
        return carry

    for c in range(CHUNKS):
        copies[2 + c].wait()
        lax.fori_loop(c * size, (c + 1) * size, add, 0, unroll=4)
    out_ref[...] = total[...].astype(BF16)


def combine(mine, dest, count, tiles, domains):
    number, block, _ = tiles.shape
    half = block // 2
    return pl.pallas_call(
        functools.partial(combine_kernel, mine),
        out_shape=jax.ShapeDtypeStruct((domains, half, block), BF16),
        in_specs=[pl.BlockSpec(memory_space=pltpu.HBM)] * 3,
        out_specs=pl.BlockSpec(memory_space=pltpu.VMEM),
        scratch_shapes=[
            pltpu.VMEM((domains, half, block), F32),
            pltpu.VMEM((number, half, block), BF16),
            pltpu.SMEM((number,), jnp.int32),
            pltpu.SMEM((number,), jnp.int32),
            pltpu.SemaphoreType.DMA((CHUNKS + 2,)),
        ],
        compiler_params=pltpu.CompilerParams(vmem_limit_bytes=VMEM_LIMIT),
        cost_estimate=SHORT,
    )(*[pltpu.with_memory_space_constraint(x, pltpu.HBM) for x in (dest, count, tiles)])


def split_kernel(group, near, own_ref, got_ref, features_ref, *outs):
    rep, _, q = place(group)
    outer = own_ref.shape[0] // group
    _, half, block = own_ref.shape
    for i, s in enumerate(near):
        for z in range(outer):
            b = z * group + lax.bitwise_xor(q, s)
            outs[i][z * half : (z + 1) * half] = (own_ref[b].astype(F32) + got_ref[b].astype(F32)).astype(BF16)
    parts = features_ref.shape[1] // 2 // block
    for i in range(parts):
        piece = features_ref[:, rows(rep * parts + i, block)]
        at = outer * half + i * block
        for s in range(1, group):
            outs[s][at : at + block] = piece


def forward_kernel(group, outer, near, far, *refs):
    own = [refs[near.index(s)] for s in range(group)]
    got = [refs[group + near.index(s)] for s in range(group)]
    features_ref, adjacency = refs[2 * group : 2 * group + 2]
    outs, panel = refs[2 * group + 2 : -1], refs[-1]
    rep, z, _ = place(group)
    block, width = features_ref.shape
    half, side = block // 2, width // 2
    for t in range(outer):
        at = pl.ds(pl.multiple_of(lax.bitwise_xor(z, t) * half, half), half)
        for s in range(group):
            columns = slice(s * block, (s + 1) * block)
            adjacency[t, rows(rep, half), columns] = own[s][at, :]
            adjacency[t, rows(1 - rep, half), columns] = got[s][at, :]
    panel[:block, :] = features_ref[:, rows(rep, side)]
    for s in range(1, group):
        for i in range(side // block):
            start = outer * half + i * block
            panel[s * block : (s + 1) * block, i * block : (i + 1) * block] = own[s][start : start + block, :]
    for i, t in enumerate(far):
        part = jnp.dot(adjacency[t], panel[...], preferred_element_type=F32)
        outs[i][...] = part.astype(outs[i].dtype)


def sum_kernel(scale, *refs):
    out = refs[-1]
    total = refs[0][...].astype(F32)
    for ref in refs[1:-1]:
        total = total + ref[...].astype(F32)
    out[...] = (total * scale if scale is not None else total).astype(out.dtype)


def dense_kernel(group, near, own_ref, got_ref, weight_ref, bias_ref, cotangent_ref, *refs):
    active_ref, row_grad_ref = refs[:2]
    outs = refs[2 : 2 + group]
    agg, pre_ref, grad, parts = refs[2 + group :]
    rep, _, q = place(group)
    width = own_ref.shape[1]
    agg[:, rows(rep, width)] = own_ref[...]
    agg[:, rows(1 - rep, width)] = got_ref[...]
    pre = jnp.dot(agg[...], weight_ref[...], preferred_element_type=F32) + bias_ref[...]
    sig = jax.nn.sigmoid(pre)
    pre_ref[...] = pre * sig
    active_ref[...] = pre_ref[:, rows(rep, width)].astype(BF16)
    slope = cotangent_ref[...].astype(F32) * sig * (1.0 + pre * (1.0 - sig))
    grad[...] = slope.astype(BF16)
    row_grad = lax.dot_general(
        grad[...], weight_ref[rows(rep, width), :], (((1,), (1,)), ((), ())), preferred_element_type=F32
    )
    row_grad_ref[...] = row_grad.astype(BF16)
    parts[...] = lax.dot_general(
        agg[...], grad[:, rows(rep, width)], (((0,), (0,)), ((), ())), preferred_element_type=F32
    )
    size = parts.shape[0] // group
    for i, s in enumerate(near):
        outs[i][...] = parts[rows(lax.bitwise_xor(q, s), size), :].astype(outs[i].dtype)


def backward_kernel(group, near, far, adjacency, *refs):
    outer, block, _ = adjacency.shape
    grads, outs = refs[:outer], refs[outer:]
    for i, s in enumerate(near):
        columns = slice(s * block, (s + 1) * block)
        total = jnp.zeros(outs[i].shape, F32)
        for j, t in enumerate(far):
            total = total + lax.dot_general(
                adjacency[t, :, columns], grads[j][...], (((0,), (0,)), ((), ())), preferred_element_type=F32
            )
        outs[i][...] = total.astype(outs[i].dtype)


def feature_kernel(*refs):
    sum_kernel(None, *refs[:-3], refs[-2])
    refs[-1][...] = refs[-3][...]


def assemble_kernel(near, *refs):
    out = refs[-1]
    _, _, q = place(len(near))
    size = refs[0].shape[0]
    for i, s in enumerate(near):
        out[rows(lax.bitwise_xor(q, s), size), :] = refs[i][...].astype(F32)


def per_device(features, tiles, tile_dest, tile_count, weight, bias, cotangent):
    domains = lax.axis_size("dom")
    group = 4
    outer = domains // group
    block, width = features.shape
    half = width // 2
    nodes = domains * block

    near = [0, group - 1, *range(1, group - 1)]
    far = [0, *range(outer // 2, outer), *range(1, outer // 2)]

    near_back, far_back = [0, *near[:0:-1]], [0, *far[:0:-1]]

    def rep_swap(x):
        return lax.ppermute(x, "rep", [(0, 1), (1, 0)])

    def inner_swap(x, s):
        return lax.ppermute(x, "dom", [(i, i ^ s) for i in range(domains)])

    def outer_swap(x, t):
        return lax.ppermute(x, "dom", [(i, i ^ (t * group)) for i in range(domains)])

    given = (tile_dest[:, 0], tile_count, tiles, domains)
    got = rep_swap(combine(False, *given))
    own = combine(True, *given)
    cut_rows = outer * block // 2
    cut = call(
        functools.partial(split_kernel, group, near),
        [((cut_rows, block), BF16)] + [((cut_rows + half, block), BF16)] * (group - 1),
        args=(own, got, features),
    )
    mine = [inner_swap(cut[i], s) if s else cut[i] for i, s in enumerate(near)]
    others = [rep_swap(x) for x in mine]
    adjacency, *parts = call(
        functools.partial(forward_kernel, group, outer, near, far),
        [((outer, block, group * block), BF16), ((block, half), F32)] + [((block, half), BF16)] * (outer - 1),
        scratch=(pltpu.VMEM((group * block, half), BF16),),
        args=(*mine, *others, features),
    )
    parts = [outer_swap(parts[i], t) if t else parts[i] for i, t in enumerate(far)]
    (agg,) = call(functools.partial(sum_kernel, None), [((block, half), BF16)], args=parts)
    active, row_grad, *pieces = call(
        functools.partial(dense_kernel, group, near),
        [((block, half), BF16), ((block, half), BF16), ((width // group, half), F32)]
        + [((width // group, half), BF16)] * (group - 1),
        scratch=(
            pltpu.VMEM((block, width), BF16),
            pltpu.VMEM((block, width), F32),
            pltpu.VMEM((block, width), BF16),
            pltpu.VMEM((width, half), F32),
        ),
        args=(agg, rep_swap(agg), weight, bias.reshape(1, width), cotangent),
    )
    pieces = [inner_swap(pieces[i], s) if s else pieces[i] for i, s in enumerate(near)]
    (piece,) = call(functools.partial(sum_kernel, None), [((width // group, half), BF16)], args=pieces)
    grads = [outer_swap(row_grad, t) if t else row_grad for t in far_back]
    back = call(
        functools.partial(backward_kernel, group, near, far_back),
        [((block, half), F32)] + [((block, half), BF16)] * (group - 1),
        args=(adjacency, *grads),
    )
    back = [inner_swap(back[i], s) if s else back[i] for i, s in enumerate(near)]
    pieces = [outer_swap(piece, t) if t else piece for t in far_back]
    (piece,) = call(
        functools.partial(sum_kernel, 1.0 / math.sqrt(nodes)), [((width // group, half), BF16)], args=pieces
    )
    pieces = [inner_swap(piece, s) if s else piece for s in near_back]
    (weight_grad,) = call(functools.partial(assemble_kernel, near_back), [((width, half), F32)], args=pieces)
    feature_grad, activated = call(
        feature_kernel, [((block, half), BF16), ((block, half), BF16)], args=(*back, active)
    )
    return (activated, weight_grad, feature_grad)


def solution(mesh):
    in_specs = (
        P("dom", None),
        P(("rep", "dom"), None, None),
        P(("rep", "dom"), None),
        P(("rep", "dom")),
        P(),
        P(),
        P("dom", None),
    )
    out_specs = (P("dom", "rep"), P(None, "rep"), P("dom", "rep"))
    return jax.shard_map(
        per_device, mesh=mesh, in_specs=in_specs, out_specs=out_specs, check_vma=False
    )
```

```python
import functools
import math

import jax
import jax.numpy as jnp
from jax import lax
from jax.experimental import pallas as pl
from jax.experimental.pallas import tpu as pltpu
from jax.sharding import PartitionSpec as P

F32, BF16 = jnp.float32, jnp.bfloat16
VMEM_LIMIT = 48 * 1024 * 1024
SHORT = pl.CostEstimate(flops=1024, bytes_accessed=1024, transcendentals=0)
CHUNKS = 4


def place(group):
    dom = lax.axis_index("dom")
    return lax.axis_index("rep"), lax.div(dom, group), lax.rem(dom, group)


def rows(start, size):
    return pl.ds(pl.multiple_of(start * size, size), size)


def call(kernel, outs, scratch=(), smem=0, args=()):
    spec = pl.BlockSpec(memory_space=pltpu.VMEM)
    return pl.pallas_call(
        kernel,
        out_shape=[jax.ShapeDtypeStruct(shape, dtype) for shape, dtype in outs],
        in_specs=[pl.BlockSpec(memory_space=pltpu.SMEM)] * smem + [spec] * (len(args) - smem),
        out_specs=[spec] * len(outs),
        scratch_shapes=list(scratch),
        compiler_params=pltpu.CompilerParams(vmem_limit_bytes=VMEM_LIMIT),
        cost_estimate=SHORT,
    )(*args)


def combine_kernel(mine, dest_hbm, count_hbm, tiles_hbm, out_ref, total, tiles, dest, count, sems):
    rep = lax.axis_index("rep")
    size = tiles.shape[0] // CHUNKS
    part = rows(rep if mine else 1 - rep, tiles.shape[1])
    copies = [
        pltpu.make_async_copy(dest_hbm, dest, sems.at[CHUNKS]),
        pltpu.make_async_copy(count_hbm, count, sems.at[CHUNKS + 1]),
    ]
    for c in range(CHUNKS):
        chunk = pl.ds(c * size, size)
        copies.append(pltpu.make_async_copy(tiles_hbm.at[chunk, part, :], tiles.at[chunk], sems.at[c]))
    for copy in copies:
        copy.start()
    total[...] = jnp.zeros_like(total)
    copies[0].wait()
    copies[1].wait()

    def add(t, carry):
        scale = lax.rsqrt(jnp.full((1, total.shape[2]), count[t], jnp.int32).astype(F32))
        d = dest[t]
        total[d] = total[d] + tiles[t].astype(F32) * scale
        return carry

    for c in range(CHUNKS):
        copies[2 + c].wait()
        lax.fori_loop(c * size, (c + 1) * size, add, 0, unroll=4)
    out_ref[...] = total[...].astype(BF16)


def combine(mine, dest, count, tiles, domains):
    number, block, _ = tiles.shape
    half = block // 2
    return pl.pallas_call(
        functools.partial(combine_kernel, mine),
        out_shape=jax.ShapeDtypeStruct((domains, half, block), BF16),
        in_specs=[pl.BlockSpec(memory_space=pltpu.HBM)] * 3,
        out_specs=pl.BlockSpec(memory_space=pltpu.VMEM),
        scratch_shapes=[
            pltpu.VMEM((domains, half, block), F32),
            pltpu.VMEM((number, half, block), BF16),
            pltpu.SMEM((number,), jnp.int32),
            pltpu.SMEM((number,), jnp.int32),
            pltpu.SemaphoreType.DMA((CHUNKS + 2,)),
        ],
        compiler_params=pltpu.CompilerParams(vmem_limit_bytes=VMEM_LIMIT),
        cost_estimate=SHORT,
    )(*[pltpu.with_memory_space_constraint(x, pltpu.HBM) for x in (dest, count, tiles)])


def half_kernel(whole_ref, out_ref):
    out_ref[...] = whole_ref[:, rows(lax.axis_index("rep"), out_ref.shape[1])]


def split_kernel(group, near, own_ref, got_ref, features_ref, *outs):
    rep, _, q = place(group)
    outer = own_ref.shape[0] // group
    _, half, block = own_ref.shape
    for i, s in enumerate(near):
        for z in range(outer):
            b = z * group + lax.bitwise_xor(q, s)
            outs[i][z * half : (z + 1) * half] = (own_ref[b].astype(F32) + got_ref[b].astype(F32)).astype(BF16)
    parts = features_ref.shape[1] // 2 // block
    for i in range(parts):
        piece = features_ref[:, rows(rep * parts + i, block)]
        at = outer * half + i * block
        for s in range(1, group):
            outs[s][at : at + block] = piece


def forward_kernel(group, outer, near, far, order, *refs):
    own = [refs[near.index(s)] for s in range(group)]
    got = [refs[group + near.index(s)] for s in range(group)]
    features_ref, adjacency = refs[2 * group], refs[-outer - 2]
    outs, panel = refs[-outer - 1 : -1], refs[-1]
    rep, z, _ = place(group)
    block, width = features_ref.shape
    half, side = block // 2, width // 2
    for i, t in enumerate(order):
        at = pl.ds(pl.multiple_of(lax.bitwise_xor(z, t) * half, half), half)
        for s in range(group):
            columns = slice(s * block, (s + 1) * block)
            adjacency[i, rows(rep, half), columns] = own[s][at, :]
            adjacency[i, rows(1 - rep, half), columns] = got[s][at, :]
    panel[:block, :] = features_ref[:, rows(rep, side)]
    for s in range(1, group):
        for i in range(side // block):
            start = outer * half + i * block
            panel[s * block : (s + 1) * block, i * block : (i + 1) * block] = own[s][start : start + block, :]
    for i, t in enumerate(far):
        part = jnp.dot(adjacency[order.index(t)], panel[...], preferred_element_type=F32)
        outs[i][...] = part.astype(outs[i].dtype)


def top_kernel(whole_ref, _, out_ref):
    out_ref[...] = whole_ref[: out_ref.shape[0], :]


def stack_kernel(number, *refs):
    for i, ref in enumerate(refs[:number]):
        refs[-1][i * ref.shape[0] : (i + 1) * ref.shape[0]] = ref[...]


def late_sum_kernel(scale, _, *refs):
    sum_kernel(scale, *refs)


def sum_kernel(scale, *refs):
    out = refs[-1]
    total = refs[0][...].astype(F32)
    for ref in refs[1:-1]:
        total = total + ref[...].astype(F32)
    out[...] = (total * scale if scale is not None else total).astype(out.dtype)


def dense_kernel(group, near, outer, place_of, *refs):
    own, got, slopes_ref = refs[:outer], refs[outer : 2 * outer], refs[2 * outer]
    weight_ref, bias_ref, active_ref, keep_ref, send_ref = refs[2 * outer + 1 : 2 * outer + 6]
    outs, (agg, grad, parts) = refs[2 * outer + 6 : -3], refs[-3:]
    rep, _, q = place(group)
    block, side = own[0].shape
    mine, other = rows(rep, side), rows(1 - rep, side)
    for t in range(outer):
        at = slice(t * block, (t + 1) * block)
        agg[at, mine] = own[t][...]
        agg[at, other] = got[t][...]
        pre = jnp.dot(agg[at, :], weight_ref[:, mine], preferred_element_type=F32) + bias_ref[:, mine]
        sig = jax.nn.sigmoid(pre)
        if t == 0:
            active_ref[...] = (pre * sig).astype(BF16)
        slope = slopes_ref[place_of[t] * block : (place_of[t] + 1) * block, :].astype(F32)
        grad[at, :] = (slope * sig * (1.0 + pre * (1.0 - sig))).astype(BF16)
    parts[...] = lax.dot_general(agg[...], grad[...], (((0,), (0,)), ((), ())), preferred_element_type=F32)
    size = parts.shape[0] // group
    for i, s in enumerate(near):
        outs[i][...] = parts[rows(lax.bitwise_xor(q, s), size), :].astype(outs[i].dtype)
    for ref, columns in ((keep_ref, mine), (send_ref, other)):
        row_grad = lax.dot_general(
            grad[...], weight_ref[columns, mine], (((1,), (1,)), ((), ())), preferred_element_type=F32
        )
        ref[...] = row_grad.astype(ref.dtype)


def backward_kernel(group, near, adjacency, keep_ref, got_ref, *refs):
    outs, grad = refs[:-1], refs[-1]
    outer, block, columns = adjacency.shape
    grad[...] = (keep_ref[...] + got_ref[...].astype(F32)).astype(BF16)
    for i, s in enumerate(near):
        total = lax.dot_general(
            adjacency[...].reshape(outer * block, columns)[:, s * block : (s + 1) * block],
            grad[...],
            (((0,), (0,)), ((), ())),
            preferred_element_type=F32,
        )
        outs[i][...] = total.astype(outs[i].dtype)


def feature_kernel(*refs):
    sum_kernel(None, *refs[:-3], refs[-2])
    refs[-1][...] = refs[-3][...]


def assemble_kernel(near, *refs):
    out = refs[-1]
    _, _, q = place(len(near))
    size = refs[0].shape[0]
    for i, s in enumerate(near):
        out[rows(lax.bitwise_xor(q, s), size), :] = refs[i][...].astype(F32)


def finish_kernel(near, *refs):
    group = len(near)
    assemble_kernel(near, *refs[:group], refs[-3])
    feature_kernel(*refs[group:-3], *refs[-2:])


def per_device(features, tiles, tile_dest, tile_count, weight, bias, cotangent):
    domains = lax.axis_size("dom")
    group = 4
    outer = domains // group
    block, width = features.shape
    half = width // 2
    nodes = domains * block

    near = [0, group - 1, *range(1, group - 1)]
    far = [0, *range(outer // 2, outer), *range(1, outer // 2)]

    near_back, far_back = [0, *near[:0:-1]], [0, *far[:0:-1]]

    def rep_swap(x):
        return lax.ppermute(x, "rep", [(0, 1), (1, 0)])

    def inner_swap(x, s):
        return lax.ppermute(x, "dom", [(i, i ^ s) for i in range(domains)])

    def outer_swap(x, t):
        return lax.ppermute(x, "dom", [(i, i ^ (t * group)) for i in range(domains)])

    given = (tile_dest[:, 0], tile_count, tiles, domains)
    got = rep_swap(combine(False, *given))
    own = combine(True, *given)
    cut_rows = outer * block // 2
    cut = call(
        functools.partial(split_kernel, group, near),
        [((cut_rows, block), BF16)] + [((cut_rows + half, block), BF16)] * (group - 1),
        args=(own, got, features),
    )
    (slopes,) = call(half_kernel, [((block, half), BF16)], args=(cotangent,))
    order, bit = [0], outer // 2
    got_slopes = outer_swap(slopes, bit)
    mine = [inner_swap(cut[i], s) if s else cut[i] for i, s in enumerate(near)]
    (last,) = call(top_kernel, [((cut_rows, block), BF16)], args=(mine[-1], got_slopes))
    others = [rep_swap(x) for x in (*mine[:-1], last)]
    adjacency, *parts = call(
        functools.partial(forward_kernel, group, outer, near, far, far_back),
        [((outer, block, group * block), BF16), ((block, half), F32)] + [((block, half), BF16)] * (outer - 1),
        scratch=(pltpu.VMEM((group * block, half), BF16),),
        args=(*mine, *others, features),
    )
    own_part = parts[0]
    parts = [outer_swap(parts[i], t) if t else parts[i] for i, t in enumerate(far)]
    while bit:
        order = order + [t ^ bit for t in order]
        (slopes,) = call(
            functools.partial(stack_kernel, 2),
            [((len(order) * block, half), BF16)],
            args=(slopes, got_slopes, own_part),
        )
        bit //= 2
        got_slopes = outer_swap(slopes, bit) if bit else None
    (agg,) = call(functools.partial(sum_kernel, None), [((block, half), BF16)], args=parts)
    aggs = [outer_swap(agg, t) if t else agg for t in far_back]
    tall = outer * block
    active, keep, send, *pieces = call(
        functools.partial(dense_kernel, group, near, outer, [order.index(t) for t in far_back]),
        [((block, half), BF16), ((tall, half), F32), ((tall, half), BF16), ((width // group, half), F32)]
        + [((width // group, half), BF16)] * (group - 1),
        scratch=(
            pltpu.VMEM((tall, width), BF16),
            pltpu.VMEM((tall, half), BF16),
            pltpu.VMEM((width, half), F32),
        ),
        args=(*aggs, *[rep_swap(x) for x in aggs], slopes, weight, bias.reshape(1, width)),
    )
    pieces = [inner_swap(pieces[i], s) if s else pieces[i] for i, s in enumerate(near)]
    back = call(
        functools.partial(backward_kernel, group, near),
        [((block, half), F32)] + [((block, half), BF16)] * (group - 1),
        scratch=(pltpu.VMEM((tall, half), BF16),),
        args=(adjacency, keep, rep_swap(send)),
    )
    back_own = back[0]
    back = [inner_swap(back[i], s) if s else back[i] for i, s in enumerate(near)]
    (piece,) = call(
        functools.partial(late_sum_kernel, 1.0 / math.sqrt(nodes)),
        [((width // group, half), BF16)],
        args=(back_own, *pieces),
    )
    pieces = [inner_swap(piece, s) if s else piece for s in near_back]
    weight_grad, feature_grad, activated = call(
        functools.partial(finish_kernel, near_back),
        [((width, half), F32), ((block, half), BF16), ((block, half), BF16)],
        args=(*pieces, *back, active),
    )
    return (activated, weight_grad, feature_grad)


def solution(mesh):
    in_specs = (
        P("dom", None),
        P(("rep", "dom"), None, None),
        P(("rep", "dom"), None),
        P(("rep", "dom")),
        P(),
        P(),
        P("dom", None),
    )
    out_specs = (P("dom", "rep"), P(None, "rep"), P("dom", "rep"))
    return jax.shard_map(
        per_device, mesh=mesh, in_specs=in_specs, out_specs=out_specs, check_vma=False
    )
```

```python
import functools
import math

import jax
import jax.numpy as jnp
from jax import lax
from jax.experimental import pallas as pl
from jax.experimental.pallas import tpu as pltpu
from jax.sharding import PartitionSpec as P

F32, BF16 = jnp.float32, jnp.bfloat16
VMEM_LIMIT = 48 * 1024 * 1024
SHORT = pl.CostEstimate(flops=1024, bytes_accessed=1024, transcendentals=0)
CHUNKS = 4


def place(group):
    dom = lax.axis_index("dom")
    return lax.axis_index("rep"), lax.div(dom, group), lax.rem(dom, group)


def rows(start, size):
    return pl.ds(pl.multiple_of(start * size, size), size)


def call(kernel, outs, scratch=(), smem=0, args=()):
    spec = pl.BlockSpec(memory_space=pltpu.VMEM)
    return pl.pallas_call(
        kernel,
        out_shape=[jax.ShapeDtypeStruct(shape, dtype) for shape, dtype in outs],
        in_specs=[pl.BlockSpec(memory_space=pltpu.SMEM)] * smem + [spec] * (len(args) - smem),
        out_specs=[spec] * len(outs),
        scratch_shapes=list(scratch),
        compiler_params=pltpu.CompilerParams(vmem_limit_bytes=VMEM_LIMIT),
        cost_estimate=SHORT,
    )(*args)


def combine_kernel(mine, dest_hbm, count_hbm, tiles_hbm, out_ref, total, tiles, dest, count, sems):
    rep = lax.axis_index("rep")
    size = tiles.shape[0] // CHUNKS
    part = rows(rep if mine else 1 - rep, tiles.shape[1])
    copies = [
        pltpu.make_async_copy(dest_hbm, dest, sems.at[CHUNKS]),
        pltpu.make_async_copy(count_hbm, count, sems.at[CHUNKS + 1]),
    ]
    for c in range(CHUNKS):
        chunk = pl.ds(c * size, size)
        copies.append(pltpu.make_async_copy(tiles_hbm.at[chunk, part, :], tiles.at[chunk], sems.at[c]))
    for copy in copies:
        copy.start()
    total[...] = jnp.zeros_like(total)
    copies[0].wait()
    copies[1].wait()

    def add(t, carry):
        scale = lax.rsqrt(jnp.full((1, total.shape[2]), count[t], jnp.int32).astype(F32))
        d = dest[t]
        total[d] = total[d] + tiles[t].astype(F32) * scale
        return carry

    for c in range(CHUNKS):
        copies[2 + c].wait()
        lax.fori_loop(c * size, (c + 1) * size, add, 0, unroll=4)
    out_ref[...] = total[...].astype(BF16)


def combine(mine, dest, count, tiles, domains):
    number, block, _ = tiles.shape
    half = block // 2
    return pl.pallas_call(
        functools.partial(combine_kernel, mine),
        out_shape=jax.ShapeDtypeStruct((domains, half, block), BF16),
        in_specs=[pl.BlockSpec(memory_space=pltpu.HBM)] * 3,
        out_specs=pl.BlockSpec(memory_space=pltpu.VMEM),
        scratch_shapes=[
            pltpu.VMEM((domains, half, block), F32),
            pltpu.VMEM((number, half, block), BF16),
            pltpu.SMEM((number,), jnp.int32),
            pltpu.SMEM((number,), jnp.int32),
            pltpu.SemaphoreType.DMA((CHUNKS + 2,)),
        ],
        compiler_params=pltpu.CompilerParams(vmem_limit_bytes=VMEM_LIMIT),
        cost_estimate=SHORT,
    )(*[pltpu.with_memory_space_constraint(x, pltpu.HBM) for x in (dest, count, tiles)])


def half_kernel(whole_ref, out_ref):
    out_ref[...] = whole_ref[:, rows(lax.axis_index("rep"), out_ref.shape[1])]


def split_kernel(group, near, own_ref, got_ref, features_ref, *outs):
    rep, _, q = place(group)
    outer = own_ref.shape[0] // group
    _, half, block = own_ref.shape
    for i, s in enumerate(near):
        for z in range(outer):
            b = z * group + lax.bitwise_xor(q, s)
            outs[i][z * half : (z + 1) * half] = (own_ref[b].astype(F32) + got_ref[b].astype(F32)).astype(BF16)
    parts = features_ref.shape[1] // 2 // block
    for i in range(parts):
        piece = features_ref[:, rows(rep * parts + i, block)]
        at = outer * half + i * block
        for s in range(1, group):
            outs[s][at : at + block] = piece


def forward_kernel(group, outer, near, far, *refs):
    own = [refs[near.index(s)] for s in range(group)]
    got = [refs[group + near.index(s)] for s in range(group)]
    features_ref, adjacency = refs[2 * group], refs[-outer - 2]
    outs, panel = refs[-outer - 1 : -1], refs[-1]
    rep, z, _ = place(group)
    block, width = features_ref.shape
    half, side = block // 2, width // 2
    for t in range(outer):
        at = slice(t * half, (t + 1) * half)
        for s in range(group):
            columns = slice(s * block, (s + 1) * block)
            adjacency[t, rows(rep, half), columns] = own[s][at, :]
            adjacency[t, rows(1 - rep, half), columns] = got[s][at, :]
    panel[:block, :] = features_ref[:, rows(rep, side)]
    for s in range(1, group):
        for i in range(side // block):
            start = outer * half + i * block
            panel[s * block : (s + 1) * block, i * block : (i + 1) * block] = own[s][start : start + block, :]
    for i, t in enumerate(far):
        part = jnp.dot(adjacency[lax.bitwise_xor(z, t)], panel[...], preferred_element_type=F32)
        outs[i][...] = part.astype(outs[i].dtype)


def top_kernel(whole_ref, _, out_ref):
    out_ref[...] = whole_ref[: out_ref.shape[0], :]


def stack_kernel(number, *refs):
    for i, ref in enumerate(refs[:number]):
        refs[-1][i * ref.shape[0] : (i + 1) * ref.shape[0]] = ref[...]


def late_sum_kernel(scale, _, *refs):
    sum_kernel(scale, *refs)


def sum_kernel(scale, *refs):
    out = refs[-1]
    total = refs[0][...].astype(F32)
    for ref in refs[1:-1]:
        total = total + ref[...].astype(F32)
    out[...] = (total * scale if scale is not None else total).astype(out.dtype)


def dense_kernel(group, near, far, place_of, *refs):
    outer = len(far)
    own, got, slopes_ref = refs[:outer], refs[outer : 2 * outer], refs[2 * outer]
    weight_ref, bias_ref, active_ref, keep_ref, send_ref = refs[2 * outer + 1 : 2 * outer + 6]
    outs, (agg, grad, parts) = refs[2 * outer + 6 : -3], refs[-3:]
    rep, z, q = place(group)
    block, side = own[0].shape
    mine, other = rows(rep, side), rows(1 - rep, side)
    for t in range(outer):
        at = rows(lax.bitwise_xor(z, far[t]), block)
        agg[at, mine] = own[t][...]
        agg[at, other] = got[t][...]
        pre = jnp.dot(agg[at, :], weight_ref[:, mine], preferred_element_type=F32) + bias_ref[:, mine]
        sig = jax.nn.sigmoid(pre)
        if t == 0:
            active_ref[...] = (pre * sig).astype(BF16)
        slope = slopes_ref[place_of[t] * block : (place_of[t] + 1) * block, :].astype(F32)
        grad[at, :] = (slope * sig * (1.0 + pre * (1.0 - sig))).astype(BF16)
    parts[...] = lax.dot_general(agg[...], grad[...], (((0,), (0,)), ((), ())), preferred_element_type=F32)
    size = parts.shape[0] // group
    for i, s in enumerate(near):
        outs[i][...] = parts[rows(lax.bitwise_xor(q, s), size), :].astype(outs[i].dtype)
    for ref, columns in ((keep_ref, mine), (send_ref, other)):
        row_grad = lax.dot_general(
            grad[...], weight_ref[columns, mine], (((1,), (1,)), ((), ())), preferred_element_type=F32
        )
        ref[...] = row_grad.astype(ref.dtype)


def backward_kernel(group, near, adjacency, keep_ref, got_ref, *refs):
    outs, grad = refs[:-1], refs[-1]
    outer, block, columns = adjacency.shape
    grad[...] = (keep_ref[...] + got_ref[...].astype(F32)).astype(BF16)
    for i, s in enumerate(near):
        total = lax.dot_general(
            adjacency[...].reshape(outer * block, columns)[:, s * block : (s + 1) * block],
            grad[...],
            (((0,), (0,)), ((), ())),
            preferred_element_type=F32,
        )
        outs[i][...] = total.astype(outs[i].dtype)


def feature_kernel(*refs):
    sum_kernel(None, *refs[:-3], refs[-2])
    refs[-1][...] = refs[-3][...]


def assemble_kernel(near, *refs):
    out = refs[-1]
    _, _, q = place(len(near))
    size = refs[0].shape[0]
    for i, s in enumerate(near):
        out[rows(lax.bitwise_xor(q, s), size), :] = refs[i][...].astype(F32)


def finish_kernel(near, *refs):
    group = len(near)
    assemble_kernel(near, *refs[:group], refs[-3])
    feature_kernel(*refs[group:-3], *refs[-2:])


def per_device(features, tiles, tile_dest, tile_count, weight, bias, cotangent):
    domains = lax.axis_size("dom")
    group = 4
    outer = domains // group
    block, width = features.shape
    half = width // 2
    nodes = domains * block

    near = [0, group - 1, *range(1, group - 1)]
    far = [0, *range(outer // 2, outer), *range(1, outer // 2)]

    near_back, far_back = [0, *near[:0:-1]], [0, *far[:0:-1]]

    def rep_swap(x):
        return lax.ppermute(x, "rep", [(0, 1), (1, 0)])

    def inner_swap(x, s):
        return lax.ppermute(x, "dom", [(i, i ^ s) for i in range(domains)])

    def outer_swap(x, t):
        return lax.ppermute(x, "dom", [(i, i ^ (t * group)) for i in range(domains)])

    given = (tile_dest[:, 0], tile_count, tiles, domains)
    got = rep_swap(combine(False, *given))
    own = combine(True, *given)
    cut_rows = outer * block // 2
    cut = call(
        functools.partial(split_kernel, group, near),
        [((cut_rows, block), BF16)] + [((cut_rows + half, block), BF16)] * (group - 1),
        args=(own, got, features),
    )
    (slopes,) = call(half_kernel, [((block, half), BF16)], args=(cotangent,))
    order, bit = [0], outer // 2
    got_slopes = outer_swap(slopes, bit)
    mine = [inner_swap(cut[i], s) if s else cut[i] for i, s in enumerate(near)]
    (last,) = call(top_kernel, [((cut_rows, block), BF16)], args=(mine[-1], got_slopes))
    others = [rep_swap(x) for x in (*mine[:-1], last)]
    adjacency, *parts = call(
        functools.partial(forward_kernel, group, outer, near, far),
        [((outer, block, group * block), BF16), ((block, half), F32)] + [((block, half), BF16)] * (outer - 1),
        scratch=(pltpu.VMEM((group * block, half), BF16),),
        args=(*mine, *others, features),
    )
    own_part = parts[0]
    parts = [outer_swap(parts[i], t) if t else parts[i] for i, t in enumerate(far)]
    while bit:
        order = order + [t ^ bit for t in order]
        (slopes,) = call(
            functools.partial(stack_kernel, 2),
            [((len(order) * block, half), BF16)],
            args=(slopes, got_slopes, own_part),
        )
        bit //= 2
        got_slopes = outer_swap(slopes, bit) if bit else None
    (agg,) = call(functools.partial(sum_kernel, None), [((block, half), BF16)], args=parts)
    aggs = [outer_swap(agg, t) if t else agg for t in far_back]
    tall = outer * block
    active, keep, send, *pieces = call(
        functools.partial(dense_kernel, group, near, far_back, [order.index(t) for t in far_back]),
        [((block, half), BF16), ((tall, half), F32), ((tall, half), BF16), ((width // group, half), F32)]
        + [((width // group, half), BF16)] * (group - 1),
        scratch=(
            pltpu.VMEM((tall, width), BF16),
            pltpu.VMEM((tall, half), BF16),
            pltpu.VMEM((width, half), F32),
        ),
        args=(*aggs, *[rep_swap(x) for x in aggs], slopes, weight, bias.reshape(1, width)),
    )
    pieces = [inner_swap(pieces[i], s) if s else pieces[i] for i, s in enumerate(near)]
    back = call(
        functools.partial(backward_kernel, group, near),
        [((block, half), F32)] + [((block, half), BF16)] * (group - 1),
        scratch=(pltpu.VMEM((tall, half), BF16),),
        args=(adjacency, keep, rep_swap(send)),
    )
    back_own = back[0]
    back = [inner_swap(back[i], s) if s else back[i] for i, s in enumerate(near)]
    (piece,) = call(
        functools.partial(late_sum_kernel, 1.0 / math.sqrt(nodes)),
        [((width // group, half), BF16)],
        args=(back_own, *pieces),
    )
    pieces = [inner_swap(piece, s) if s else piece for s in near_back]
    weight_grad, feature_grad, activated = call(
        functools.partial(finish_kernel, near_back),
        [((width, half), F32), ((block, half), BF16), ((block, half), BF16)],
        args=(*pieces, *back, active),
    )
    return (activated, weight_grad, feature_grad)


def solution(mesh):
    in_specs = (
        P("dom", None),
        P(("rep", "dom"), None, None),
        P(("rep", "dom"), None),
        P(("rep", "dom")),
        P(),
        P(),
        P("dom", None),
    )
    out_specs = (P("dom", "rep"), P(None, "rep"), P("dom", "rep"))
    return jax.shard_map(
        per_device, mesh=mesh, in_specs=in_specs, out_specs=out_specs, check_vma=False
    )
```

```python
import functools
import math

import jax
import jax.numpy as jnp
from jax import lax
from jax.experimental import pallas as pl
from jax.experimental.pallas import tpu as pltpu
from jax.sharding import PartitionSpec as P

F32, BF16 = jnp.float32, jnp.bfloat16
VMEM_LIMIT = 48 * 1024 * 1024
SHORT = pl.CostEstimate(flops=1024, bytes_accessed=1024, transcendentals=0)
CHUNKS = 4


def place(group):
    dom = lax.axis_index("dom")
    return lax.axis_index("rep"), lax.div(dom, group), lax.rem(dom, group)


def rows(start, size):
    return pl.ds(pl.multiple_of(start * size, size), size)


def call(kernel, outs, scratch=(), smem=0, args=()):
    spec = pl.BlockSpec(memory_space=pltpu.VMEM)
    return pl.pallas_call(
        kernel,
        out_shape=[jax.ShapeDtypeStruct(shape, dtype) for shape, dtype in outs],
        in_specs=[pl.BlockSpec(memory_space=pltpu.SMEM)] * smem + [spec] * (len(args) - smem),
        out_specs=[spec] * len(outs),
        scratch_shapes=list(scratch),
        compiler_params=pltpu.CompilerParams(vmem_limit_bytes=VMEM_LIMIT),
        cost_estimate=SHORT,
    )(*args)


def combine_kernel(mine, dest_hbm, count_hbm, tiles_hbm, out_ref, total, tiles, dest, count, sems):
    rep = lax.axis_index("rep")
    size = tiles.shape[0] // CHUNKS
    part = rows(rep if mine else 1 - rep, tiles.shape[1])
    copies = [
        pltpu.make_async_copy(dest_hbm, dest, sems.at[CHUNKS]),
        pltpu.make_async_copy(count_hbm, count, sems.at[CHUNKS + 1]),
    ]
    for c in range(CHUNKS):
        chunk = pl.ds(c * size, size)
        copies.append(pltpu.make_async_copy(tiles_hbm.at[chunk, part, :], tiles.at[chunk], sems.at[c]))
    for copy in copies:
        copy.start()
    total[...] = jnp.zeros_like(total)
    copies[0].wait()
    copies[1].wait()

    def add(t, carry):
        scale = lax.rsqrt(jnp.full((1, total.shape[2]), count[t], jnp.int32).astype(F32))
        d = dest[t]
        total[d] = total[d] + tiles[t].astype(F32) * scale
        return carry

    for c in range(CHUNKS):
        copies[2 + c].wait()
        lax.fori_loop(c * size, (c + 1) * size, add, 0, unroll=4)
    out_ref[...] = total[...].astype(BF16)


def combine(mine, dest, count, tiles, domains):
    number, block, _ = tiles.shape
    half = block // 2
    return pl.pallas_call(
        functools.partial(combine_kernel, mine),
        out_shape=jax.ShapeDtypeStruct((domains, half, block), BF16),
        in_specs=[pl.BlockSpec(memory_space=pltpu.HBM)] * 3,
        out_specs=pl.BlockSpec(memory_space=pltpu.VMEM),
        scratch_shapes=[
            pltpu.VMEM((domains, half, block), F32),
            pltpu.VMEM((number, half, block), BF16),
            pltpu.SMEM((number,), jnp.int32),
            pltpu.SMEM((number,), jnp.int32),
            pltpu.SemaphoreType.DMA((CHUNKS + 2,)),
        ],
        compiler_params=pltpu.CompilerParams(vmem_limit_bytes=VMEM_LIMIT),
        cost_estimate=SHORT,
    )(*[pltpu.with_memory_space_constraint(x, pltpu.HBM) for x in (dest, count, tiles)])


def half_kernel(whole_ref, out_ref):
    out_ref[...] = whole_ref[:, rows(lax.axis_index("rep"), out_ref.shape[1])]


def split_kernel(group, near, own_ref, got_ref, features_ref, *outs):
    rep, _, q = place(group)
    outer = own_ref.shape[0] // group
    _, half, block = own_ref.shape
    for i, s in enumerate(near):
        for z in range(outer):
            b = z * group + lax.bitwise_xor(q, s)
            outs[i][z * half : (z + 1) * half] = (own_ref[b].astype(F32) + got_ref[b].astype(F32)).astype(BF16)
    parts = features_ref.shape[1] // 2 // block
    for i in range(parts):
        piece = features_ref[:, rows(rep * parts + i, block)]
        at = outer * half + i * block
        for s in range(1, group):
            outs[s][at : at + block] = piece


def forward_kernel(group, outer, near, far, *refs):
    own = [refs[near.index(s)] for s in range(group)]
    got = [refs[group + near.index(s)] for s in range(group)]
    features_ref, adjacency = refs[2 * group], refs[-outer - 2]
    outs, panel = refs[-outer - 1 : -1], refs[-1]
    rep, z, _ = place(group)
    block, width = features_ref.shape
    half, side = block // 2, width // 2
    for t in range(outer):
        at = slice(t * half, (t + 1) * half)
        for s in range(group):
            columns = slice(s * block, (s + 1) * block)
            adjacency[t, rows(rep, half), columns] = own[s][at, :]
            adjacency[t, rows(1 - rep, half), columns] = got[s][at, :]
    panel[:block, :] = features_ref[:, rows(rep, side)]
    for s in range(1, group):
        for i in range(side // block):
            start = outer * half + i * block
            panel[s * block : (s + 1) * block, i * block : (i + 1) * block] = own[s][start : start + block, :]
    for i, t in enumerate(far):
        part = jnp.dot(adjacency[lax.bitwise_xor(z, t)], panel[...], preferred_element_type=F32)
        outs[i][...] = part.astype(outs[i].dtype)


def top_kernel(whole_ref, _, out_ref):
    out_ref[...] = whole_ref[: out_ref.shape[0], :]


def stack_kernel(number, *refs):
    for i, ref in enumerate(refs[:number]):
        refs[-1][i * ref.shape[0] : (i + 1) * ref.shape[0]] = ref[...]


def late_sum_kernel(scale, _, *refs):
    sum_kernel(scale, *refs)


def sum_kernel(scale, *refs):
    out = refs[-1]
    total = refs[0][...].astype(F32)
    for ref in refs[1:-1]:
        total = total + ref[...].astype(F32)
    out[...] = (total * scale if scale is not None else total).astype(out.dtype)


def dense_kernel(group, near, far, place_of, *refs):
    outer = len(far)
    own, got, slopes_ref = refs[:outer], refs[outer : 2 * outer], refs[2 * outer]
    weight_ref, bias_ref, active_ref, keep_ref, send_ref = refs[2 * outer + 1 : 2 * outer + 6]
    outs, (agg, grad, parts) = refs[2 * outer + 6 : -3], refs[-3:]
    rep, z, q = place(group)
    block, side = own[0].shape
    mine, other = rows(rep, side), rows(1 - rep, side)
    for t in range(outer):
        at = rows(lax.bitwise_xor(z, far[t]), block)
        agg[at, mine] = own[t][...]
        agg[at, other] = got[t][...]
        pre = jnp.dot(agg[at, :], weight_ref[:, mine], preferred_element_type=F32) + bias_ref[:, mine]
        sig = jax.nn.sigmoid(pre)
        if t == 0:
            active_ref[...] = (pre * sig).astype(BF16)
        slope = slopes_ref[place_of[t] * block : (place_of[t] + 1) * block, :].astype(F32)
        grad[at, :] = (slope * sig * (1.0 + pre * (1.0 - sig))).astype(BF16)
    parts[...] = lax.dot_general(agg[...], grad[...], (((0,), (0,)), ((), ())), preferred_element_type=F32)
    size = parts.shape[0] // group
    for i, s in enumerate(near):
        outs[i][...] = parts[rows(lax.bitwise_xor(q, s), size), :].astype(outs[i].dtype)
    for ref, columns in ((keep_ref, mine), (send_ref, other)):
        row_grad = lax.dot_general(
            grad[...], weight_ref[columns, mine], (((1,), (1,)), ((), ())), preferred_element_type=F32
        )
        ref[...] = row_grad.astype(ref.dtype)


def backward_kernel(group, near, adjacency, keep_ref, got_ref, *refs):
    outs, grad = refs[:-1], refs[-1]
    outer, block, columns = adjacency.shape
    grad[...] = (keep_ref[...] + got_ref[...].astype(F32)).astype(BF16)
    for i, s in enumerate(near):
        total = lax.dot_general(
            adjacency[...].reshape(outer * block, columns)[:, s * block : (s + 1) * block],
            grad[...],
            (((0,), (0,)), ((), ())),
            preferred_element_type=F32,
        )
        outs[i][...] = total.astype(outs[i].dtype)


def feature_kernel(*refs):
    sum_kernel(None, *refs[:-3], refs[-2])
    refs[-1][...] = refs[-3][...]


def assemble_kernel(near, *refs):
    out = refs[-1]
    _, _, q = place(len(near))
    size = refs[0].shape[0]
    for i, s in enumerate(near):
        out[rows(lax.bitwise_xor(q, s), size), :] = refs[i][...].astype(F32)


def finish_kernel(near, *refs):
    group = len(near)
    assemble_kernel(near, *refs[:group], refs[-3])
    feature_kernel(*refs[group:-3], *refs[-2:])


def per_device(features, tiles, tile_dest, tile_count, weight, bias, cotangent):
    domains = lax.axis_size("dom")
    group = 4
    outer = domains // group
    block, width = features.shape
    half = width // 2
    nodes = domains * block

    near, near_back = [0, group - 1, *range(1, group - 1)], [0, *range(group - 2, 0, -1), group - 1]
    blocks_near = [0, 1, *range(group - 1, 1, -1)]
    far, far_back = [0, *range(outer - 1, 0, -1)], [0, *range(2, 0, -1), *range(3, outer)]

    def rep_swap(x):
        return lax.ppermute(x, "rep", [(0, 1), (1, 0)])

    def inner_swap(x, s):
        return lax.ppermute(x, "dom", [(i, i ^ s) for i in range(domains)])

    def outer_swap(x, t):
        return lax.ppermute(x, "dom", [(i, i ^ (t * group)) for i in range(domains)])

    given = (tile_dest[:, 0], tile_count, tiles, domains)
    got = rep_swap(combine(False, *given))
    own = combine(True, *given)
    cut_rows = outer * block // 2
    cut = call(
        functools.partial(split_kernel, group, near),
        [((cut_rows, block), BF16)] + [((cut_rows + half, block), BF16)] * (group - 1),
        args=(own, got, features),
    )
    (slopes,) = call(half_kernel, [((block, half), BF16)], args=(cotangent,))
    order, bit = [0], outer // 2
    got_slopes = outer_swap(slopes, bit)
    mine = [inner_swap(cut[i], s) if s else cut[i] for i, s in enumerate(near)]
    (last,) = call(top_kernel, [((cut_rows, block), BF16)], args=(mine[-1], got_slopes))
    others = [rep_swap(x) for x in (*mine[:-1], last)]
    adjacency, *parts = call(
        functools.partial(forward_kernel, group, outer, near, far),
        [((outer, block, group * block), BF16), ((block, half), F32)] + [((block, half), BF16)] * (outer - 1),
        scratch=(pltpu.VMEM((group * block, half), BF16),),
        args=(*mine, *others, features),
    )
    own_part = parts[0]
    parts = [outer_swap(parts[i], t) if t else parts[i] for i, t in enumerate(far)]
    while bit:
        order = order + [t ^ bit for t in order]
        (slopes,) = call(
            functools.partial(stack_kernel, 2),
            [((len(order) * block, half), BF16)],
            args=(slopes, got_slopes, own_part),
        )
        bit //= 2
        got_slopes = outer_swap(slopes, bit) if bit else None
    (agg,) = call(functools.partial(sum_kernel, None), [((block, half), BF16)], args=parts)
    aggs = [outer_swap(agg, t) if t else agg for t in far_back]
    tall = outer * block
    active, keep, send, *pieces = call(
        functools.partial(dense_kernel, group, near, far_back, [order.index(t) for t in far_back]),
        [((block, half), BF16), ((tall, half), F32), ((tall, half), BF16), ((width // group, half), F32)]
        + [((width // group, half), BF16)] * (group - 1),
        scratch=(
            pltpu.VMEM((tall, width), BF16),
            pltpu.VMEM((tall, half), BF16),
            pltpu.VMEM((width, half), F32),
        ),
        args=(*aggs, *[rep_swap(x) for x in aggs], slopes, weight, bias.reshape(1, width)),
    )
    pieces = [inner_swap(pieces[i], s) if s else pieces[i] for i, s in enumerate(near)]
    back = call(
        functools.partial(backward_kernel, group, blocks_near),
        [((block, half), F32)] + [((block, half), BF16)] * (group - 1),
        scratch=(pltpu.VMEM((tall, half), BF16),),
        args=(adjacency, keep, rep_swap(send)),
    )
    back_own = back[0]
    back = [inner_swap(back[i], s) if s else back[i] for i, s in enumerate(blocks_near)]
    (piece,) = call(
        functools.partial(late_sum_kernel, 1.0 / math.sqrt(nodes)),
        [((width // group, half), BF16)],
        args=(back_own, *pieces),
    )
    pieces = [inner_swap(piece, s) if s else piece for s in near_back]
    weight_grad, feature_grad, activated = call(
        functools.partial(finish_kernel, near_back),
        [((width, half), F32), ((block, half), BF16), ((block, half), BF16)],
        args=(*pieces, *back, active),
    )
    return (activated, weight_grad, feature_grad)


def solution(mesh):
    in_specs = (
        P("dom", None),
        P(("rep", "dom"), None, None),
        P(("rep", "dom"), None),
        P(("rep", "dom")),
        P(),
        P(),
        P("dom", None),
    )
    out_specs = (P("dom", "rep"), P(None, "rep"), P("dom", "rep"))
    return jax.shard_map(
        per_device, mesh=mesh, in_specs=in_specs, out_specs=out_specs, check_vma=False
    )
```

```python
import functools
import math

import jax
import jax.numpy as jnp
from jax import lax
from jax.experimental import pallas as pl
from jax.experimental.pallas import tpu as pltpu
from jax.sharding import PartitionSpec as P

F32, BF16 = jnp.float32, jnp.bfloat16
VMEM_LIMIT = 48 * 1024 * 1024
SHORT = pl.CostEstimate(flops=1024, bytes_accessed=1024, transcendentals=0)
CHUNKS = 4


def place(group):
    dom = lax.axis_index("dom")
    return lax.axis_index("rep"), lax.div(dom, group), lax.rem(dom, group)


def rows(start, size):
    return pl.ds(pl.multiple_of(start * size, size), size)


def call(kernel, outs, scratch=(), smem=0, args=()):
    spec = pl.BlockSpec(memory_space=pltpu.VMEM)
    return pl.pallas_call(
        kernel,
        out_shape=[jax.ShapeDtypeStruct(shape, dtype) for shape, dtype in outs],
        in_specs=[pl.BlockSpec(memory_space=pltpu.SMEM)] * smem + [spec] * (len(args) - smem),
        out_specs=[spec] * len(outs),
        scratch_shapes=list(scratch),
        compiler_params=pltpu.CompilerParams(vmem_limit_bytes=VMEM_LIMIT),
        cost_estimate=SHORT,
    )(*args)


def combine_kernel(mine, dest_hbm, count_hbm, tiles_hbm, out_ref, total, tiles, dest, count, sems):
    rep = lax.axis_index("rep")
    size = tiles.shape[0] // CHUNKS
    part = rows(rep if mine else 1 - rep, tiles.shape[1])
    copies = [
        pltpu.make_async_copy(dest_hbm, dest, sems.at[CHUNKS]),
        pltpu.make_async_copy(count_hbm, count, sems.at[CHUNKS + 1]),
    ]
    for c in range(CHUNKS):
        chunk = pl.ds(c * size, size)
        copies.append(pltpu.make_async_copy(tiles_hbm.at[chunk, part, :], tiles.at[chunk], sems.at[c]))
    for copy in copies:
        copy.start()
    total[...] = jnp.zeros_like(total)
    copies[0].wait()
    copies[1].wait()

    def add(t, carry):
        scale = lax.rsqrt(jnp.full((1, total.shape[2]), count[t], jnp.int32).astype(F32))
        d = dest[t]
        total[d] = total[d] + tiles[t].astype(F32) * scale
        return carry

    for c in range(CHUNKS):
        copies[2 + c].wait()
        lax.fori_loop(c * size, (c + 1) * size, add, 0, unroll=4)
    out_ref[...] = total[...].astype(BF16)


def combine(mine, dest, count, tiles, domains):
    number, block, _ = tiles.shape
    half = block // 2
    return pl.pallas_call(
        functools.partial(combine_kernel, mine),
        out_shape=jax.ShapeDtypeStruct((domains, half, block), BF16),
        in_specs=[pl.BlockSpec(memory_space=pltpu.HBM)] * 3,
        out_specs=pl.BlockSpec(memory_space=pltpu.VMEM),
        scratch_shapes=[
            pltpu.VMEM((domains, half, block), F32),
            pltpu.VMEM((number, half, block), BF16),
            pltpu.SMEM((number,), jnp.int32),
            pltpu.SMEM((number,), jnp.int32),
            pltpu.SemaphoreType.DMA((CHUNKS + 2,)),
        ],
        compiler_params=pltpu.CompilerParams(vmem_limit_bytes=VMEM_LIMIT),
        cost_estimate=SHORT,
    )(*[pltpu.with_memory_space_constraint(x, pltpu.HBM) for x in (dest, count, tiles)])


def half_kernel(whole_ref, out_ref):
    out_ref[...] = whole_ref[:, rows(lax.axis_index("rep"), out_ref.shape[1])]


def split_kernel(group, near, own_ref, got_ref, features_ref, *outs):
    rep, _, q = place(group)
    outer = own_ref.shape[0] // group
    _, half, block = own_ref.shape
    for i, s in enumerate(near):
        for z in range(outer):
            b = z * group + lax.bitwise_xor(q, s)
            outs[i][z * half : (z + 1) * half] = (own_ref[b].astype(F32) + got_ref[b].astype(F32)).astype(BF16)
    parts = features_ref.shape[1] // 2 // block
    for i in range(parts):
        piece = features_ref[:, rows(rep * parts + i, block)]
        at = outer * half + i * block
        for s in range(1, group):
            outs[s][at : at + block] = piece


def begin_kernel(outer, *refs):
    number = (len(refs) - 4) // 2
    own, got, features_ref = refs[:number], refs[number : 2 * number], refs[2 * number]
    adjacency, partial, panel = refs[2 * number + 1 :]
    rep, _, _ = place(number + 1)
    block, width = features_ref.shape
    half, side = block // 2, width // 2
    panel[:block, :] = features_ref[:, rows(rep, side)]
    for k in range(number):
        columns = slice(k * block, (k + 1) * block)
        for t in range(outer):
            at = slice(t * half, (t + 1) * half)
            adjacency[t, rows(rep, half), columns] = own[k][at, :]
            adjacency[t, rows(1 - rep, half), columns] = got[k][at, :]
        for i in range(side // block if k else 0):
            start = outer * half + i * block
            panel[columns, i * block : (i + 1) * block] = own[k][start : start + block, :]
    for t in range(outer):
        partial[t] = jnp.dot(adjacency[t], panel[...], preferred_element_type=F32)


def forward_kernel(group, far, own_ref, got_ref, partial, adjacency, *refs):
    outs, panel = refs[:-1], refs[-1]
    rep, z, _ = place(group)
    outer, block, side = partial.shape
    half = block // 2
    for t in range(outer):
        at = slice(t * half, (t + 1) * half)
        adjacency[t, rows(rep, half), :] = own_ref[at, :]
        adjacency[t, rows(1 - rep, half), :] = got_ref[at, :]
    for i in range(side // block):
        start = outer * half + i * block
        panel[:, i * block : (i + 1) * block] = own_ref[start : start + block, :]
    for i, t in enumerate(far):
        b = lax.bitwise_xor(z, t)
        part = partial[b] + jnp.dot(adjacency[b], panel[...], preferred_element_type=F32)
        outs[i][...] = part.astype(outs[i].dtype)


def top_kernel(whole_ref, _, out_ref):
    out_ref[...] = whole_ref[: out_ref.shape[0], :]


def stack_kernel(number, *refs):
    for i, ref in enumerate(refs[:number]):
        refs[-1][i * ref.shape[0] : (i + 1) * ref.shape[0]] = ref[...]


def late_sum_kernel(scale, _, *refs):
    sum_kernel(scale, *refs)


def sum_kernel(scale, *refs):
    out = refs[-1]
    total = refs[0][...].astype(F32)
    for ref in refs[1:-1]:
        total = total + ref[...].astype(F32)
    out[...] = (total * scale if scale is not None else total).astype(out.dtype)


def dense_kernel(group, near, far, place_of, *refs):
    outer = len(far)
    own, got, slopes_ref = refs[:outer], refs[outer : 2 * outer], refs[2 * outer]
    weight_ref, bias_ref, active_ref, keep_ref, send_ref = refs[2 * outer + 1 : 2 * outer + 6]
    outs, (agg, grad, parts) = refs[2 * outer + 6 : -3], refs[-3:]
    rep, z, q = place(group)
    block, side = own[0].shape
    mine, other = rows(rep, side), rows(1 - rep, side)
    for t in range(outer):
        at = rows(lax.bitwise_xor(z, far[t]), block)
        agg[at, mine] = own[t][...]
        agg[at, other] = got[t][...]
        pre = jnp.dot(agg[at, :], weight_ref[:, mine], preferred_element_type=F32) + bias_ref[:, mine]
        sig = jax.nn.sigmoid(pre)
        if t == 0:
            active_ref[...] = (pre * sig).astype(BF16)
        slope = slopes_ref[place_of[t] * block : (place_of[t] + 1) * block, :].astype(F32)
        grad[at, :] = (slope * sig * (1.0 + pre * (1.0 - sig))).astype(BF16)
    parts[...] = lax.dot_general(agg[...], grad[...], (((0,), (0,)), ((), ())), preferred_element_type=F32)
    size = parts.shape[0] // group
    for i, s in enumerate(near):
        outs[i][...] = parts[rows(lax.bitwise_xor(q, s), size), :].astype(outs[i].dtype)
    for ref, columns in ((keep_ref, mine), (send_ref, other)):
        row_grad = lax.dot_general(
            grad[...], weight_ref[columns, mine], (((1,), (1,)), ((), ())), preferred_element_type=F32
        )
        ref[...] = row_grad.astype(ref.dtype)


def backward_kernel(near, held, first, final, keep_ref, got_ref, *refs):
    outs, grad = refs[:-1], refs[-1]
    outer, block, _ = final.shape
    grad[...] = (keep_ref[...] + got_ref[...].astype(F32)).astype(BF16)
    for i, s in enumerate(near):
        k = held.index(s)
        strip = final[...] if s == held[-1] else first[:, :, k * block : (k + 1) * block]
        total = lax.dot_general(
            strip.reshape(outer * block, block),
            grad[...],
            (((0,), (0,)), ((), ())),
            preferred_element_type=F32,
        )
        outs[i][...] = total.astype(outs[i].dtype)


def feature_kernel(*refs):
    sum_kernel(None, *refs[:-3], refs[-2])
    refs[-1][...] = refs[-3][...]


def assemble_kernel(near, *refs):
    out = refs[-1]
    _, _, q = place(len(near))
    size = refs[0].shape[0]
    for i, s in enumerate(near):
        out[rows(lax.bitwise_xor(q, s), size), :] = refs[i][...].astype(F32)


def finish_kernel(near, *refs):
    group = len(near)
    assemble_kernel(near, *refs[:group], refs[-3])
    feature_kernel(*refs[group:-3], *refs[-2:])


def per_device(features, tiles, tile_dest, tile_count, weight, bias, cotangent):
    domains = lax.axis_size("dom")
    group = 4
    outer = domains // group
    block, width = features.shape
    half = width // 2
    nodes = domains * block

    near, near_back = [0, group - 1, *range(1, group - 1)], [0, *range(group - 2, 0, -1), group - 1]
    blocks_near = [0, 1, *range(group - 1, 1, -1)]
    far, far_back = [0, *range(outer - 1, 0, -1)], [0, *range(2, 0, -1), *range(3, outer)]

    def rep_swap(x):
        return lax.ppermute(x, "rep", [(0, 1), (1, 0)])

    def inner_swap(x, s):
        return lax.ppermute(x, "dom", [(i, i ^ s) for i in range(domains)])

    def outer_swap(x, t):
        return lax.ppermute(x, "dom", [(i, i ^ (t * group)) for i in range(domains)])

    given = (tile_dest[:, 0], tile_count, tiles, domains)
    got = rep_swap(combine(False, *given))
    own = combine(True, *given)
    cut_rows = outer * block // 2
    cut = call(
        functools.partial(split_kernel, group, near),
        [((cut_rows, block), BF16)] + [((cut_rows + half, block), BF16)] * (group - 1),
        args=(own, got, features),
    )
    (slopes,) = call(half_kernel, [((block, half), BF16)], args=(cotangent,))
    order, bit = [0], outer // 2
    got_slopes = outer_swap(slopes, bit)
    mine = [inner_swap(cut[i], s) if s else cut[i] for i, s in enumerate(near)]
    (last,) = call(top_kernel, [((cut_rows, block), BF16)], args=(mine[-1], got_slopes))
    others = [rep_swap(x) for x in (*mine[:-1], last)]
    first, partial = call(
        functools.partial(begin_kernel, outer),
        [((outer, block, (group - 1) * block), BF16), ((outer, block, half), F32)],
        scratch=(pltpu.VMEM(((group - 1) * block, half), BF16),),
        args=(*mine[:-1], *others[:-1], features),
    )
    final, *parts = call(
        functools.partial(forward_kernel, group, far),
        [((outer, block, block), BF16), ((block, half), F32)] + [((block, half), BF16)] * (outer - 1),
        scratch=(pltpu.VMEM((block, half), BF16),),
        args=(mine[-1], others[-1], partial),
    )
    own_part = parts[0]
    parts = [outer_swap(parts[i], t) if t else parts[i] for i, t in enumerate(far)]
    while bit:
        order = order + [t ^ bit for t in order]
        (slopes,) = call(
            functools.partial(stack_kernel, 2),
            [((len(order) * block, half), BF16)],
            args=(slopes, got_slopes, own_part),
        )
        bit //= 2
        got_slopes = outer_swap(slopes, bit) if bit else None
    (agg,) = call(functools.partial(sum_kernel, None), [((block, half), BF16)], args=parts)
    aggs = [outer_swap(agg, t) if t else agg for t in far_back]
    tall = outer * block
    active, keep, send, *pieces = call(
        functools.partial(dense_kernel, group, near, far_back, [order.index(t) for t in far_back]),
        [((block, half), BF16), ((tall, half), F32), ((tall, half), BF16), ((width // group, half), F32)]
        + [((width // group, half), BF16)] * (group - 1),
        scratch=(
            pltpu.VMEM((tall, width), BF16),
            pltpu.VMEM((tall, half), BF16),
            pltpu.VMEM((width, half), F32),
        ),
        args=(*aggs, *[rep_swap(x) for x in aggs], slopes, weight, bias.reshape(1, width)),
    )
    pieces = [inner_swap(pieces[i], s) if s else pieces[i] for i, s in enumerate(near)]
    back = call(
        functools.partial(backward_kernel, blocks_near, near),
        [((block, half), F32)] + [((block, half), BF16)] * (group - 1),
        scratch=(pltpu.VMEM((tall, half), BF16),),
        args=(first, final, keep, rep_swap(send)),
    )
    back_own = back[0]
    back = [inner_swap(back[i], s) if s else back[i] for i, s in enumerate(blocks_near)]
    (piece,) = call(
        functools.partial(late_sum_kernel, 1.0 / math.sqrt(nodes)),
        [((width // group, half), BF16)],
        args=(back_own, *pieces),
    )
    pieces = [inner_swap(piece, s) if s else piece for s in near_back]
    weight_grad, feature_grad, activated = call(
        functools.partial(finish_kernel, near_back),
        [((width, half), F32), ((block, half), BF16), ((block, half), BF16)],
        args=(*pieces, *back, active),
    )
    return (activated, weight_grad, feature_grad)


def solution(mesh):
    in_specs = (
        P("dom", None),
        P(("rep", "dom"), None, None),
        P(("rep", "dom"), None),
        P(("rep", "dom")),
        P(),
        P(),
        P("dom", None),
    )
    out_specs = (P("dom", "rep"), P(None, "rep"), P("dom", "rep"))
    return jax.shard_map(
        per_device, mesh=mesh, in_specs=in_specs, out_specs=out_specs, check_vma=False
    )
```
